128 devices in a mesh: expert: 16 (over z, y_hi, core), dp: 8 (over x, y_lo).
Axes of the slice: x: 4, y: 4 (y_hi: 2, y_lo: 2; y = y_hi * 2 + y_lo), z: 4, core: 2. Of those that a mesh axis runs over, the one named last changes fastest.
Arguments:
- tokens: bfloat16 [16384, 2048], P(('expert', 'dp')), may hold values from -6 to 6
- route_weights: float32 [16384, 2], P(('expert', 'dp')), may hold values from 0.1 to 1
- assignment: int32 [16384, 2], P(('expert', 'dp')), may hold values from 0 to 15, all different within a row; in each aligned block of 128 rows (0 to 127, 128 to 255, ...) at most 32 rows name the same one
- out_grad: bfloat16 [16384, 2048], P(('expert', 'dp')), may hold values from -6 to 6
- weights: bfloat16 [16, 3, 2048, 768], P('expert'), may hold values from -0.125 to 0.125
- first_moment: bfloat16 [16, 3, 2048, 768], P('expert', None, 'dp'), may hold values from -12 to 12
- second_moment: bfloat16 [16, 3, 2048, 768], P('expert', None, 'dp'), may hold values from 1 to 400
- partner: int32 [16], replicated, may hold values from 0 to 15, as said below
Outputs:
- moe_out: bfloat16 [16384, 2048], P(('expert', 'dp'))
- token_grads: bfloat16 [16384, 2048], P(('expert', 'dp'))
- route_grads: float32 [16384, 2], P(('expert', 'dp'))
- new_weights: bfloat16 [16, 3, 2048, 768], P('expert', None, 'dp')
- new_first: bfloat16 [16, 3, 2048, 768], P('expert', None, 'dp')
- new_second: bfloat16 [16, 3, 2048, 768], P('expert', None, 'dp')
The draws below stay inside these ranges and needn't reach their ends.
Inputs may be any that keep to these rules, and one draw needn't show every extreme that they name: `assignment`: among the tokens of one device (aligned blocks of 128 rows) at most 32 rows name any one expert, and one expert is named by exactly 32 rows in some blocks; a row names 2 different experts. partner[e] is e XOR one nonzero number that is the same for all e, so experts trade slots in pairs.
All inputs are finite; a program needn't handle non-finite values.
Results may differ from the reference program's by a relative error of at most 0.025.
Values may be sent and summed in bfloat16 or wider, within the bound.
A program may use at most 128 MiB of HBM per device.

```python
import math
import jax
import jax.numpy as jnp
import numpy as np
from jax import lax

D = 2048
FF = 768
TOPK = 2
TOK_DEV = 128
EXPERTS = 16
CAP = 32
TOKENS = 16384
N_EXPERT = 16
N_DP = 8
DEVICES = 128


def draw_partner(key, part):
    common = jax.random.randint(key, (), 1, EXPERTS, dtype=jnp.int32)
    return jnp.bitwise_xor(jnp.arange(EXPERTS, dtype=jnp.int32), common).astype(jnp.int32)


def shard_levels(rng, dims, shards, least, largest):
    def one(axis_at, shards_of):
        steps = jax.random.uniform(jax.random.fold_in(jax.random.fold_in(rng, 6), axis_at), (shards_of,), jnp.float32, least / len(shards), largest / len(shards))
        return jnp.repeat(jnp.exp(steps), dims[axis_at] // shards_of).reshape((-1,) + (1,) * (len(dims) - axis_at - 1))

    gain = one(*shards[0])
    for cut in shards[1:]:
        gain = gain * one(*cut)
    return gain


def shared_out(own_key, own, number, rows, number_of, top, most, slope):
    ranking = jax.random.permutation(own_key, number_of)
    packed, ordinary = portions_of(number_of, rows * top, most, slope, True), portions_of(number_of, rows * top, most, slope, False)
    places = jnp.arange(number_of)

    def named(sizes, turn):
        used = int((sizes > 0).sum())
        fixed = max(1, used // 4)
        passed = fixed + (places - fixed + turn * (used - fixed)) % max(1, number_of - fixed)
        return jnp.zeros((number_of,), jnp.int32).at[ranking[jnp.where(places < fixed, places, passed)]].set(jnp.asarray(sizes, jnp.int32))

    sizes = jnp.where(number % 4 == 0, named(packed, number // 4), named(ordinary, number - number // 4 - 1))
    mixed = jax.random.permutation(jax.random.fold_in(own, 3), number_of)
    source_of, sink = mixed[0:number_of // 2 * 2:2], mixed[1:number_of // 2 * 2:2]
    margin = jnp.minimum(sizes[source_of] - 1, most - sizes[sink]) // 2
    margin = jnp.where((source_of == ranking[0]) | (sink == ranking[0]) | (sizes[sink] == 0), 0, jnp.maximum(margin, 0))
    passed = jax.random.randint(jax.random.fold_in(own, 4), (number_of // 2,), 0, 1 << 20) % (margin + 1)
    sizes = sizes.at[source_of].add(-passed).at[sink].add(passed)
    items = jnp.searchsorted(jnp.cumsum(sizes), jnp.arange(rows * top), side="right").astype(jnp.int32)
    grid = items.reshape(top, rows).T
    grid = grid[jax.random.permutation(jax.random.fold_in(own, 1), rows)]
    turn = jax.random.randint(jax.random.fold_in(own, 2), (rows, 1), 0, top)
    return jnp.take_along_axis(grid, (jnp.arange(top)[None, :] + turn) % top, axis=1)


def portions_of(amount, total, limit, skew, full):
    portions = [(1 << 20) // math.isqrt(grade ** skew) + 1 for grade in range(1, amount + 1)]
    largest = limit if full else min(limit, max(-(-total // amount), total * portions[0] // sum(portions)))
    least = 1 if total - largest >= amount - 1 else 0
    counts, spare = [largest] + [least] * (amount - 1), total - largest - least * (amount - 1)
    while spare > 0:
        candidates = [i for i in range(1, amount) if counts[i] < largest] or [i for i in range(1, amount) if counts[i] < limit]
        mass, budget = sum([portions[i] for i in candidates]), spare
        for i in candidates:
            more = min(limit - counts[i], max(1, budget * portions[i] // mass), spare)
            counts[i] = counts[i] + more
            spare = spare - more
    return np.array(counts)


def gaussian(key, shape, width, limit, cuts=(), held_as=jnp.bfloat16):
    values = jax.random.normal(key, shape, jnp.float32) * width
    if len(cuts) > 0:
        values = shard_levels(key, shape, cuts, -0.22, 0.18) * values
    return jnp.clip(values, min=-limit, max=limit).astype(held_as)


def setup_inputs(seed: int = 0) -> dict:
    streams_of = jax.random.split(jax.random.key(seed), 9)
    tokens = gaussian(streams_of[0], (TOKENS, D), 1.0, 6.0, ((0, 128),))
    route_weights = jnp.clip(0.1 + 0.9 * jax.random.uniform(streams_of[1], (TOKENS, TOPK), jnp.float32) ** shard_levels(streams_of[1], (TOKENS, TOPK), ((0, 128),), -0.2, 0.2), 0.1, 1.0)
    assignment_keys = jax.random.split(jax.random.fold_in(streams_of[2], 1), TOKENS // TOK_DEV)
    assignment_turns = jax.random.permutation(jax.random.fold_in(streams_of[2], 3), TOKENS // TOK_DEV)
    assignment = jax.vmap(lambda own, number: shared_out(jax.random.fold_in(streams_of[2], 2), own, number, TOK_DEV, EXPERTS, TOPK, CAP, 2))(assignment_keys, assignment_turns).reshape((TOKENS, TOPK))
    out_grad = gaussian(streams_of[3], (TOKENS, D), 1.0, 6.0, ((0, 128),))
    weights = gaussian(streams_of[4], (EXPERTS, 3, D, FF), D ** -0.5, 0.125, ((0, 16),))
    first_moment = gaussian(streams_of[5], (EXPERTS, 3, D, FF), 2.0, 12.0, ((0, 16), (2, 8)))
    second_moment = jnp.clip(jnp.exp(math.log(400.0) - 5.9914645 * jax.random.uniform(streams_of[6], (EXPERTS, 3, D, FF), jnp.float32) ** shard_levels(streams_of[6], (EXPERTS, 3, D, FF), ((0, 16), (2, 8)), -0.2, 0.2)), 1.0, 400.0).astype(jnp.bfloat16)
    partner = draw_partner(jax.random.fold_in(streams_of[8], 71), 0)
    return dict(tokens=tokens, route_weights=route_weights, assignment=assignment, out_grad=out_grad, weights=weights, first_moment=first_moment, second_moment=second_moment, partner=partner)


beta_first = 0.9
beta_second = 0.95
learn_rate = 0.001
weight_decay = 0.1
adam_epsilon = 1e-08
first_fix = 0.9999734386011124
second_fix = 0.994079470779666

def adamw(weight_piece, first_moment, second_moment, gradient):
    first_new = beta_first * first_moment.astype(jnp.float32) + (1.0 - beta_first) * gradient
    second_new = beta_second * second_moment.astype(jnp.float32) + (1.0 - beta_second) * gradient * gradient
    weight_full = weight_piece.astype(jnp.float32)
    update = first_new / first_fix / (jnp.sqrt(second_new / second_fix) + adam_epsilon) + weight_decay * weight_full
    return ((weight_full - learn_rate * update).astype(jnp.bfloat16), first_new.astype(jnp.bfloat16), second_new.astype(jnp.bfloat16))

def expert_pass(rows, grad_rows, weight):
    gate_act = jnp.dot(rows, weight[0], preferred_element_type=jnp.float32)
    up_act = jnp.dot(rows, weight[1], preferred_element_type=jnp.float32)
    sigmoid_gate = jax.nn.sigmoid(gate_act)
    silu_gate = gate_act * sigmoid_gate
    hidden = (silu_gate * up_act).astype(jnp.bfloat16)
    expert_out = jnp.dot(hidden, weight[2].T, preferred_element_type=jnp.float32).astype(jnp.bfloat16)
    hidden_grad = jnp.dot(grad_rows, weight[2], preferred_element_type=jnp.float32)
    gate_grad = (hidden_grad * up_act * sigmoid_gate * (1.0 + gate_act * (1.0 - sigmoid_gate))).astype(jnp.bfloat16)
    up_grad = (hidden_grad * silu_gate).astype(jnp.bfloat16)
    row_grads = (jnp.dot(gate_grad, weight[0].T, preferred_element_type=jnp.float32) + jnp.dot(up_grad, weight[1].T, preferred_element_type=jnp.float32)).astype(jnp.bfloat16)
    return (expert_out, row_grads, hidden, gate_grad, up_grad)

def reference(tokens, route_weights, assignment, out_grad, weights, first_moment, second_moment, partner):
    chosen = assignment.reshape(-1).astype(jnp.int32)
    pair_count = chosen.shape[0]
    blocks = chosen.reshape(DEVICES, TOK_DEV * TOPK)
    onehot = (blocks[:, :, None] == jnp.arange(EXPERTS, dtype=jnp.int32)[None, None, :]).astype(jnp.int32)
    earlier = jnp.cumsum(onehot, axis=1) - onehot
    ranks = lax.optimization_barrier(jnp.sum(earlier * onehot, axis=2))
    device_ids = jnp.arange(DEVICES, dtype=jnp.int32)[:, None]
    buffer_rows = N_DP * N_EXPERT * CAP
    position = ((device_ids % N_DP * N_EXPERT + device_ids // N_DP) * CAP + ranks).reshape(-1).astype(jnp.int32)
    pair_ids = jnp.arange(pair_count, dtype=jnp.int32)
    weight_flat = route_weights.reshape(-1)

    def shaped(values):
        return values.reshape(N_DP, N_EXPERT * CAP, values.shape[-1]).astype(jnp.float32)

    def one_expert(expert_id):
        target = jnp.where(chosen == expert_id, position, buffer_rows).astype(jnp.int32)
        source = jnp.full((buffer_rows,), -1, jnp.int32).at[target].set(pair_ids, mode='drop')
        present = (source >= 0)[:, None]
        safe_pair = jnp.maximum(source, 0).astype(jnp.int32)
        token_ids = (safe_pair // TOPK).astype(jnp.int32)
        rows = jnp.where(present, tokens[token_ids], jnp.zeros((), jnp.bfloat16))
        scaled = (weight_flat[safe_pair][:, None] * out_grad[token_ids].astype(jnp.float32)).astype(jnp.bfloat16)
        grad_rows = jnp.where(present, scaled, jnp.zeros((), jnp.bfloat16))
        weight = weights[expert_id]
        expert_out, row_grads, hidden, gate_grad, up_grad = expert_pass(rows, grad_rows, weight)
        part_gate = jnp.einsum('nrd,nrf->ndf', shaped(rows), shaped(gate_grad))
        part_up = jnp.einsum('nrd,nrf->ndf', shaped(rows), shaped(up_grad))
        part_down = jnp.einsum('nrd,nrf->ndf', shaped(grad_rows), shaped(hidden))
        partial_grads = lax.optimization_barrier(jnp.stack([part_gate, part_up, part_down], axis=1).astype(jnp.bfloat16))
        gradient = lax.optimization_barrier(jnp.sum(partial_grads.astype(jnp.float32), axis=0))
        updated, first_new, second_new = adamw(weight, first_moment[expert_id], second_moment[expert_id], gradient)
        return (expert_out, row_grads, updated, first_new, second_new)
    outputs, row_all, updated, first_new, second_new = lax.map(one_expert, jnp.arange(EXPERTS, dtype=jnp.int32))
    pair_out = outputs[chosen, position].reshape(TOKENS, TOPK, D).astype(jnp.float32)
    moe_out = lax.optimization_barrier(jnp.sum(route_weights[:, :, None] * pair_out, axis=1)).astype(jnp.bfloat16)
    route_grads = lax.optimization_barrier(jnp.sum(out_grad.astype(jnp.float32)[:, None, :] * pair_out, axis=2))
    pair_grads = row_all[chosen, position].reshape(TOKENS, TOPK, D).astype(jnp.float32)
    token_grads = lax.optimization_barrier(jnp.sum(pair_grads, axis=1)).astype(jnp.bfloat16)
    return (moe_out, token_grads, route_grads, updated[partner], first_new[partner], second_new[partner])
```

```python
import functools

import jax
import jax.numpy as jnp
from jax import lax
from jax.experimental import pallas as pl
from jax.experimental.pallas import tpu as pltpu
from jax.sharding import PartitionSpec as P

beta_first = 0.9
beta_second = 0.95
learn_rate = 0.001
weight_decay = 0.1
adam_epsilon = 1e-08
first_fix = 0.9999734386011124
second_fix = 0.994079470779666

MESH = pl.DeviceIdType.MESH
F32 = jnp.float32
BF16 = jnp.bfloat16
LANES = 128
NZ, NY, NC = 4, 2, 2
NX = 4
PLANE = NY * NC


def dot(a, b, ca=1, cb=0):
    return lax.dot_general(a, b, (((ca,), (cb,)), ((), ())), preferred_element_type=F32)


def pair_slots(assign_ref, capacity):
    tok = assign_ref.shape[0]
    lane = lax.broadcasted_iota(jnp.int32, (tok, LANES), 1)
    named = [(assign_ref[:, k : k + 1] == lane).astype(F32) for k in range(2)]
    below = (
        lax.broadcasted_iota(jnp.int32, (tok, tok), 0)
        > lax.broadcasted_iota(jnp.int32, (tok, tok), 1)
    ).astype(F32)
    earlier = dot(below.astype(BF16), (named[0] + named[1]).astype(BF16))
    return [
        assign_ref[:, k : k + 1] * capacity
        + jnp.sum(earlier * named[k], axis=1, keepdims=True).astype(jnp.int32)
        for k in range(2)
    ]


def rem(a, n):
    return lax.rem(a, jnp.int32(n))


def div(a, n):
    return lax.div(a, jnp.int32(n))


def rows_at(index, size):
    return pl.ds(pl.multiple_of(index * size, size), size)


def expert_coords():
    me = lax.axis_index("expert").astype(jnp.int32)
    return me, div(me, PLANE), rem(div(me, NC), NY), rem(me, NC)


def expert_peers():
    me, z, y, core = expert_coords()
    out = []
    for dz in (2, 1, 3, 0):
        for dy in (1, 0):
            for dc in (0, 1):
                if (dz, dy, dc) != (0, 0, 0):
                    out.append(
                        rem(z + dz, NZ) * PLANE + rem(y + dy, NY) * NC + rem(core + dc, NC)
                    )
    return out


def expert_kernel(
    capacity,
    assign_ref,
    rw_ref,
    tok_ref,
    og_ref,
    w_hbm,
    eo_out,
    rg_out,
    pg_out,
    scaled,
    send_rows,
    send_grads,
    rows_in,
    grads_in,
    w,
    coef_gate,
    coef_up,
    hidden,
    gate_grad,
    up_grad,
    eo,
    rg,
    pg,
    w_sem,
    rows_s,
    rows_r,
    grads_s,
    grads_r,
    out_sem,
):
    me, z, y, core = expert_coords()
    tok, width = tok_ref.shape
    ff = w.shape[2]
    chunk = PLANE * capacity
    peers = expert_peers()
    barrier = pltpu.get_barrier_semaphore()
    for peer in peers:
        pl.semaphore_signal(barrier, inc=1, device_id={"expert": peer}, device_id_type=MESH)
    w_copies = [pltpu.make_async_copy(w_hbm.at[0, p], w.at[p], w_sem.at[p]) for p in range(3)]
    for copy in w_copies:
        copy.start()

    slot = pair_slots(assign_ref, capacity)
    slot_lane = lax.broadcasted_iota(jnp.int32, (tok, chunk), 1)
    for k in range(2):
        scaled[k * tok : (k + 1) * tok, :] = (
            rw_ref[:, k : k + 1] * og_ref[...].astype(F32)
        ).astype(BF16)

    def sent(buffer, target, sems_s, sems_r, peer):
        return pltpu.make_async_remote_copy(
            src_ref=buffer.at[rows_at(peer, capacity)],
            dst_ref=target.at[rows_at(me, capacity)],
            send_sem=sems_s.at[peer],
            recv_sem=sems_r.at[me],
            device_id={"expert": peer},
            device_id_type=MESH,
        )

    def own(buffer, target, sems_r):
        return pltpu.make_async_copy(
            buffer.at[rows_at(me, capacity)], target.at[rows_at(me, capacity)], sems_r.at[me]
        )

    def came(buffer, target, sems_s, sems_r, source):
        return pltpu.make_async_remote_copy(
            src_ref=buffer.at[rows_at(source, capacity)],
            dst_ref=target.at[rows_at(source, capacity)],
            send_sem=sems_s.at[source],
            recv_sem=sems_r.at[source],
            device_id={"expert": source},
            device_id_type=MESH,
        )

    def onehots(plane):
        return [(slot[k] - plane * chunk == slot_lane).astype(F32).astype(BF16) for k in range(2)]

    first = True
    at = 0
    for dz in (2, 1, 3, 0):
        plane = rem(z + dz, NZ)
        hot = onehots(plane)
        send_rows[rows_at(plane, chunk), :] = dot(hot[0] + hot[1], tok_ref[...], 0, 0).astype(BF16)
        if first:
            pl.semaphore_wait(barrier, len(peers))
            first = False
        count = PLANE - (dz == 0)
        for peer in peers[at : at + count]:
            sent(send_rows, rows_in, rows_s, rows_r, peer).start()
        at += count
    own(send_rows, rows_in, rows_r).start()
    at = 0
    for dz in (2, 1, 3, 0):
        plane = rem(z + dz, NZ)
        hot = jnp.concatenate(onehots(plane), axis=0)
        send_grads[rows_at(plane, chunk), :] = dot(hot, scaled[...], 0, 0).astype(BF16)
        count = PLANE - (dz == 0)
        for peer in peers[at : at + count]:
            sent(send_grads, grads_in, grads_s, grads_r, peer).start()
        at += count
    own(send_grads, grads_in, grads_r).start()

    for copy in w_copies:
        copy.wait()

    def plane_of(step):
        half = div(step, 2)
        return rem(z + step + half * (1 - 2 * rem(step, 2)), NZ)

    def forward(step, carry):
        plane = plane_of(step)
        for j in range(PLANE):
            came(send_rows, rows_in, rows_s, rows_r, plane * PLANE + j).wait_recv()
        at_rows = rows_at(plane, chunk)
        rows = rows_in[at_rows, :]
        gate = dot(rows, w[0])
        up = dot(rows, w[1])
        sig = jax.nn.sigmoid(gate)
        silu = gate * sig
        hid = (silu * up).astype(BF16)
        hidden[at_rows, :] = hid
        coef_up[at_rows, :] = silu
        coef_gate[at_rows, :] = up * sig * (1.0 + gate * (1.0 - sig))
        eo[at_rows, :] = dot(hid, w[2], 1, 1).astype(BF16)
        return carry

    lax.fori_loop(0, NZ, forward, 0)
    eo_copy = pltpu.make_async_copy(eo, eo_out, out_sem.at[0])
    eo_copy.start()

    def backward(step, carry):
        plane = plane_of(step)
        for j in range(PLANE):
            came(send_grads, grads_in, grads_s, grads_r, plane * PLANE + j).wait_recv()
        at_rows = rows_at(plane, chunk)
        hidden_grad = dot(grads_in[at_rows, :], w[2])
        gate_grad[at_rows, :] = (hidden_grad * coef_gate[at_rows, :]).astype(BF16)
        up_grad[at_rows, :] = (hidden_grad * coef_up[at_rows, :]).astype(BF16)
        return carry

    lax.fori_loop(0, NZ, backward, 0)

    tile = 256
    pg_copies = []
    for p, (left, right) in enumerate(
        ((rows_in, gate_grad), (rows_in, up_grad), (grads_in, hidden))
    ):

        def weight_tile(j, carry, left=left, right=right, p=p):
            at_cols = rows_at(j, tile)
            pg[p, at_cols, :] = dot(left[:, at_cols], right[...], 0, 0).astype(BF16)
            return carry

        lax.fori_loop(0, width // tile, weight_tile, 0)
        copy = pltpu.make_async_copy(pg.at[p], pg_out.at[p], out_sem.at[1 + p])
        copy.start()
        pg_copies.append(copy)

    def row_tile(j, carry):
        at_cols = rows_at(j, tile)
        rg[:, at_cols] = (
            dot(gate_grad[...], w[0, at_cols, :], 1, 1) + dot(up_grad[...], w[1, at_cols, :], 1, 1)
        ).astype(BF16)
        return carry

    lax.fori_loop(0, width // tile, row_tile, 0)
    rg_copy = pltpu.make_async_copy(rg, rg_out, out_sem.at[4])
    rg_copy.start()
    for peer in peers:
        sent(send_rows, rows_in, rows_s, rows_r, peer).wait_send()
        sent(send_grads, grads_in, grads_s, grads_r, peer).wait_send()
    for copy in (eo_copy, *pg_copies, rg_copy):
        copy.wait()


def reduce_kernel(
    capacity,
    assign_ref,
    rw_ref,
    og_ref,
    eo_hbm,
    rg_hbm,
    pg_hbm,
    w_hbm,
    m_ref,
    v_ref,
    moe_ref,
    tg_ref,
    route_ref,
    new_ref,
    ret_eo,
    ret_rg,
    one_l,
    one_r,
    two_l,
    two_r,
    mine_p,
    mine_m,
    mine,
    sum_p,
    sum_m,
    y_out,
    y_in,
    w_own,
    eo_s,
    eo_r,
    rg_s,
    rg_r,
    x_s,
    x_r,
    y_s,
    y_r,
    loc_sem,
):
    me, z, y, core = expert_coords()
    d = lax.axis_index("dp").astype(jnp.int32)
    x, yl = div(d, 2), rem(d, 2)
    tok, width = og_ref.shape
    half = m_ref.shape[2]
    ff = m_ref.shape[3]
    xp, xm, xo = rem(x + 1, NX), rem(x + NX - 1, NX), rem(x + 2, NX)
    right, left, beside = {"dp": xp * 2 + yl}, {"dp": xm * 2 + yl}, {"dp": x * 2 + 1 - yl}
    peers = expert_peers()
    barrier = pltpu.get_barrier_semaphore()
    for target in [{"expert": peer} for peer in peers] + [right, left, beside]:
        pl.semaphore_signal(barrier, inc=1, device_id=target, device_id_type=MESH)

    def part(p, xx, h):
        return pg_hbm.at[p, rows_at(xx * 2 + h, half)]

    local = []

    def bring(src, dst):
        copy = pltpu.make_async_copy(src, dst, loc_sem.at[len(local)])
        copy.start()
        local.append(copy)

    for p in range(3):
        bring(part(p, xp, 0), mine_p.at[p])
        bring(part(p, xm, 1), mine_m.at[p])
    for p in range(3):
        bring(part(p, x, 0), mine.at[p, 0])
        bring(part(p, x, 1), mine.at[p, 1])
    for p in range(3):
        bring(w_hbm.at[0, p, rows_at(d, half)], w_own.at[p])

    pl.semaphore_wait(barrier, len(peers) + 3)

    def put(src, dst, sems_s, sems_r, index, target):
        return pltpu.make_async_remote_copy(
            src_ref=src,
            dst_ref=dst,
            send_sem=sems_s.at[index],
            recv_sem=sems_r.at[index],
            device_id=target,
            device_id_type=MESH,
        )

    one = [
        (
            put(part(p, xo, 0), one_l.at[p], x_s, x_r, 6 * p, right),
            put(part(p, xo, 1), one_r.at[p], x_s, x_r, 6 * p + 1, left),
        )
        for p in range(3)
    ]
    alone = [
        (
            put(part(p, xp, 1), two_l.at[p, 1], x_s, x_r, 6 * p + 2, right),
            put(part(p, xm, 0), two_r.at[p, 0], x_s, x_r, 6 * p + 3, left),
        )
        for p in range(3)
    ]
    both = [
        (
            put(sum_p.at[p], two_l.at[p, 0], x_s, x_r, 6 * p + 4, right),
            put(sum_m.at[p], two_r.at[p, 1], x_s, x_r, 6 * p + 5, left),
        )
        for p in range(3)
    ]
    across = [put(y_out.at[p], y_in.at[p], y_s, y_r, p, beside) for p in range(3)]
    for p in range(3):
        for copy in one[p]:
            copy.start()

    def returned(source, target, sems_s, sems_r, peer):
        return pltpu.make_async_remote_copy(
            src_ref=source.at[rows_at(peer, capacity)],
            dst_ref=target.at[rows_at(me, capacity)],
            send_sem=sems_s.at[peer],
            recv_sem=sems_r.at[me],
            device_id={"expert": peer},
            device_id_type=MESH,
        )

    def came(source, target, sems_s, sems_r, peer):
        return pltpu.make_async_remote_copy(
            src_ref=source.at[rows_at(peer, capacity)],
            dst_ref=target.at[rows_at(peer, capacity)],
            send_sem=sems_s.at[peer],
            recv_sem=sems_r.at[peer],
            device_id={"expert": peer},
            device_id_type=MESH,
        )

    homes = ((eo_hbm, ret_eo, eo_s, eo_r), (rg_hbm, ret_rg, rg_s, rg_r))
    owns = []
    for source, target, sems_s, sems_r in homes:
        for peer in peers:
            returned(source, target, sems_s, sems_r, peer).start()
        copy = pltpu.make_async_copy(
            source.at[rows_at(me, capacity)], target.at[rows_at(me, capacity)], sems_r.at[me]
        )
        copy.start()
        owns.append(copy)
    for p in range(3):
        for copy in alone[p]:
            copy.start()

    for copy in local:
        copy.wait()
    block = 32
    steps = half // block
    for p in range(3):
        for copy in one[p]:
            copy.wait_recv()

        def add(i, carry, p=p):
            at = rows_at(i, block)
            sum_p[p, at, :] = (mine_p[p, at, :].astype(F32) + one_l[p, at, :].astype(F32)).astype(BF16)
            sum_m[p, at, :] = (mine_m[p, at, :].astype(F32) + one_r[p, at, :].astype(F32)).astype(BF16)
            return carry

        lax.fori_loop(0, steps, add, 0)
        for copy in both[p]:
            copy.start()

    slot = pair_slots(assign_ref, capacity)
    slots = ret_eo.shape[0]
    slot_lane = lax.broadcasted_iota(jnp.int32, (tok, slots), 1)
    hot = [(slot[k] == slot_lane).astype(F32).astype(BF16) for k in range(2)]
    hot_both = jnp.concatenate(hot, axis=0)
    hot_sum = hot[0] + hot[1]
    tile = 512
    rw = [rw_ref[:, k : k + 1] for k in range(2)]
    for peer in peers:
        came(*homes[0], peer).wait_recv()
    owns[0].wait()

    def combine(j, route):
        at = rows_at(j, tile)
        pairs = dot(hot_both, ret_eo[:, at])
        first, second = pairs[:tok], pairs[tok:]
        moe_ref[:, at] = (rw[0] * first + rw[1] * second).astype(BF16)
        grad = og_ref[:, at].astype(F32)
        return (
            route[0] + jnp.sum(grad * first, axis=1, keepdims=True),
            route[1] + jnp.sum(grad * second, axis=1, keepdims=True),
        )

    zero = jnp.zeros((tok, 1), F32)
    route = lax.fori_loop(0, width // tile, combine, (zero, zero))
    route_ref[:, 0:1] = route[0]
    route_ref[:, 1:2] = route[1]
    for peer in peers:
        came(*homes[1], peer).wait_recv()
    owns[1].wait()

    def combine_grads(j, carry):
        at = rows_at(j, tile)
        tg_ref[:, at] = dot(hot_sum, ret_rg[:, at]).astype(BF16)
        return carry

    lax.fori_loop(0, width // tile, combine_grads, 0)

    def total(p, h, at):
        return (
            mine[p, h, at, :].astype(F32)
            + two_l[p, h, at, :].astype(F32)
            + two_r[p, h, at, :].astype(F32)
        )

    for p in range(3):
        for copy in (*alone[p], *both[p]):
            copy.wait_recv()

        def sum_other(i, carry, p=p):
            at = rows_at(i, block)
            y_out[p, at, :] = total(p, 1 - yl, at).astype(BF16)
            return carry

        lax.fori_loop(0, steps, sum_other, 0)
        across[p].start()

    for p in range(3):
        across[p].wait_recv()

        def adamw(i, carry, p=p):
            at = rows_at(i, block)
            grad = total(p, yl, at) + y_in[p, at, :].astype(F32)
            first_new = beta_first * m_ref[0, p, at, :].astype(F32) + (1.0 - beta_first) * grad
            second_new = (
                beta_second * v_ref[0, p, at, :].astype(F32) + (1.0 - beta_second) * grad * grad
            )
            full = w_own[p, at, :].astype(F32)
            update = (
                first_new * (1.0 / first_fix)
                / (jnp.sqrt(second_new * (1.0 / second_fix)) + adam_epsilon)
                + weight_decay * full
            )
            new_ref[0, p, at, :] = (full - learn_rate * update).astype(BF16)
            new_ref[1, p, at, :] = first_new.astype(BF16)
            new_ref[2, p, at, :] = second_new.astype(BF16)
            return carry

        lax.fori_loop(0, steps, adamw, 0)

    for p in range(3):
        for copy in (*one[p], *alone[p], *both[p], across[p]):
            copy.wait_send()
    for source, target, sems_s, sems_r in homes:
        for peer in peers:
            returned(source, target, sems_s, sems_r, peer).wait_send()


def move(mask, stacked, count):
    return lax.ppermute(stacked, "expert", [(i, i ^ mask) for i in range(count)])


def per_device(
    tokens, route_weights, assignment, out_grad, weights, first_moment, second_moment, partner
):
    experts = lax.axis_size("expert")
    tok, topk = assignment.shape
    width = tokens.shape[1]
    capacity = 2 * tok * topk // experts
    slots = experts * capacity
    ff = weights.shape[3]
    half = first_moment.shape[2]
    vmem = pl.BlockSpec(memory_space=pltpu.VMEM)
    anywhere = pl.BlockSpec(memory_space=pl.ANY)
    dma = pltpu.SemaphoreType.DMA
    shape = jax.ShapeDtypeStruct
    eo, rg, pg = pl.pallas_call(
        functools.partial(expert_kernel, capacity),
        out_shape=(
            shape((slots, width), BF16),
            shape((slots, width), BF16),
            shape((3, width, ff), BF16),
        ),
        in_specs=[vmem] * 4 + [anywhere],
        out_specs=(anywhere,) * 3,
        scratch_shapes=[
            pltpu.VMEM((topk * tok, width), BF16),
            pltpu.VMEM((slots, width), BF16),
            pltpu.VMEM((slots, width), BF16),
            pltpu.VMEM((slots, width), BF16),
            pltpu.VMEM((slots, width), BF16),
            pltpu.VMEM((3, width, ff), BF16),
            pltpu.VMEM((slots, ff), F32),
            pltpu.VMEM((slots, ff), F32),
            pltpu.VMEM((slots, ff), BF16),
            pltpu.VMEM((slots, ff), BF16),
            pltpu.VMEM((slots, ff), BF16),
            pltpu.VMEM((slots, width), BF16),
            pltpu.VMEM((slots, width), BF16),
            pltpu.VMEM((3, width, ff), BF16),
            dma((3,)),
            dma((experts,)),
            dma((experts,)),
            dma((experts,)),
            dma((experts,)),
            dma((5,)),
        ],
        compiler_params=pltpu.CompilerParams(
            collective_id=0, has_side_effects=True, vmem_limit_bytes=56 * 2**20
        ),
    )(assignment, route_weights, tokens, out_grad, weights)
    piece = (3, half, ff)
    moe_out, token_grads, route_grads, new = pl.pallas_call(
        functools.partial(reduce_kernel, capacity),
        out_shape=(
            shape((tok, width), BF16),
            shape((tok, width), BF16),
            shape((tok, topk), F32),
            shape((3,) + piece, BF16),
        ),
        in_specs=[vmem] * 3 + [anywhere] * 4 + [vmem] * 2,
        out_specs=(vmem,) * 4,
        scratch_shapes=[
            pltpu.VMEM((slots, width), BF16),
            pltpu.VMEM((slots, width), BF16),
            pltpu.VMEM(piece, BF16),
            pltpu.VMEM(piece, BF16),
            pltpu.VMEM((3, 2, half, ff), BF16),
            pltpu.VMEM((3, 2, half, ff), BF16),
            pltpu.VMEM(piece, BF16),
            pltpu.VMEM(piece, BF16),
            pltpu.VMEM((3, 2, half, ff), BF16),
            pltpu.VMEM(piece, BF16),
            pltpu.VMEM(piece, BF16),
            pltpu.VMEM(piece, BF16),
            pltpu.VMEM(piece, BF16),
            pltpu.VMEM(piece, BF16),
            dma((experts,)),
            dma((experts,)),
            dma((experts,)),
            dma((experts,)),
            dma((18,)),
            dma((18,)),
            dma((3,)),
            dma((3,)),
            dma((15,)),
        ],
        compiler_params=pltpu.CompilerParams(
            collective_id=1, has_side_effects=True, vmem_limit_bytes=56 * 2**20
        ),
    )(assignment, route_weights, out_grad, eo, rg, pg, weights, first_moment, second_moment)
    moved = lax.switch(
        partner[0] - 1,
        [functools.partial(move, mask, count=experts) for mask in range(1, experts)],
        new,
    )
    return (moe_out, token_grads, route_grads, moved[0:1], moved[1:2], moved[2:3])


def solution(mesh):
    placed = (
        P(("expert", "dp"), None),
        P(("expert", "dp"), None),
        P(("expert", "dp"), None),
        P(("expert", "dp"), None),
        P("expert", None, None, None),
        P("expert", None, "dp", None),
        P("expert", None, "dp", None),
        P(),
    )
    return jax.shard_map(
        per_device,
        mesh=mesh,
        in_specs=placed,
        out_specs=(
            P(("expert", "dp"), None),
            P(("expert", "dp"), None),
            P(("expert", "dp"), None),
            P("expert", None, "dp", None),
            P("expert", None, "dp", None),
            P("expert", None, "dp", None),
        ),
        check_vma=False,
    )
```

```python
import functools

import jax
import jax.numpy as jnp
from jax import lax
from jax.experimental import pallas as pl
from jax.experimental.pallas import tpu as pltpu
from jax.sharding import PartitionSpec as P

beta_first = 0.9
beta_second = 0.95
learn_rate = 0.001
weight_decay = 0.1
adam_epsilon = 1e-08
first_fix = 0.9999734386011124
second_fix = 0.994079470779666

MESH = pl.DeviceIdType.MESH
F32 = jnp.float32
BF16 = jnp.bfloat16
LANES = 128
NZ, NY, NC = 4, 2, 2
NX = 4
PLANE = NY * NC


def dot(a, b, ca=1, cb=0):
    return lax.dot_general(a, b, (((ca,), (cb,)), ((), ())), preferred_element_type=F32)


def pair_slots(assign_ref, capacity):
    tok = assign_ref.shape[0]
    lane = lax.broadcasted_iota(jnp.int32, (tok, LANES), 1)
    named = [(assign_ref[:, k : k + 1] == lane).astype(F32) for k in range(2)]
    below = (
        lax.broadcasted_iota(jnp.int32, (tok, tok), 0)
        > lax.broadcasted_iota(jnp.int32, (tok, tok), 1)
    ).astype(F32)
    earlier = dot(below.astype(BF16), (named[0] + named[1]).astype(BF16))
    return [
        assign_ref[:, k : k + 1] * capacity
        + jnp.sum(earlier * named[k], axis=1, keepdims=True).astype(jnp.int32)
        for k in range(2)
    ]


def rem(a, n):
    return lax.rem(a, jnp.int32(n))


def div(a, n):
    return lax.div(a, jnp.int32(n))


def rows_at(index, size):
    return pl.ds(pl.multiple_of(index * size, size), size)


def expert_coords():
    me = lax.axis_index("expert").astype(jnp.int32)
    return me, div(me, PLANE), rem(div(me, NC), NY), rem(me, NC)


def expert_peers():
    me, z, y, core = expert_coords()
    out = []
    for dz in (2, 1, 3, 0):
        for dy in (1, 0):
            for dc in (0, 1):
                if (dz, dy, dc) != (0, 0, 0):
                    out.append(
                        rem(z + dz, NZ) * PLANE + rem(y + dy, NY) * NC + rem(core + dc, NC)
                    )
    return out


def layer_kernel(
    capacity,
    chunks,
    partner_ref,
    assign_ref,
    rw_ref,
    tok_ref,
    og_ref,
    w_hbm,
    m_ref,
    v_ref,
    moe_ref,
    tg_ref,
    route_ref,
    moved,
    scaled,
    send_rows,
    send_grads,
    rows_in,
    grads_in,
    w,
    coef_gate,
    coef_up,
    hidden,
    gate_grad,
    up_grad,
    pg,
    ret_eo,
    ret_rg,
    one_l,
    one_r,
    two_l,
    two_r,
    y_in,
    *rest,
):
    count = len(chunks)
    stages, mids = rest[:count], rest[count : 2 * count]
    (
        w_sem,
        rows_s,
        rows_r,
        grads_s,
        grads_r,
        eo_s,
        eo_r,
        rg_s,
        rg_r,
        x_s,
        x_r,
        y_s,
        y_r,
        out_s,
        out_r,
        home_s,
        home_r,
    ) = rest[2 * count :]
    me, z, y, core = expert_coords()
    d = lax.axis_index("dp").astype(jnp.int32)
    x, yl = div(d, 2), rem(d, 2)
    xp, xm, xo = rem(x + 1, NX), rem(x + NX - 1, NX), rem(x + 2, NX)
    right, left, beside = {"dp": xp * 2 + yl}, {"dp": xm * 2 + yl}, {"dp": x * 2 + 1 - yl}
    tok, width = tok_ref.shape
    experts = stages[0].shape[0]
    half = m_ref.shape[2]
    chunk = PLANE * capacity
    peers = expert_peers()
    barrier = pltpu.get_barrier_semaphore()
    for target in [{"expert": peer} for peer in peers] + [right, left, beside]:
        pl.semaphore_signal(barrier, inc=1, device_id=target, device_id_type=MESH)
    w_copies = [pltpu.make_async_copy(w_hbm.at[0, p], w.at[p], w_sem.at[p]) for p in range(3)]
    for copy in w_copies:
        copy.start()

    slot = pair_slots(assign_ref, capacity)
    slot_lane = lax.broadcasted_iota(jnp.int32, (tok, chunk), 1)

    def put(src, dst, sem_s, sem_r, target):
        return pltpu.make_async_remote_copy(
            src_ref=src,
            dst_ref=dst,
            send_sem=sem_s,
            recv_sem=sem_r,
            device_id=target,
            device_id_type=MESH,
        )

    class Swap:
        def __init__(self, source, target, sems_s, sems_r, base=0):
            self.source, self.target = source, target
            self.sems_s, self.sems_r, self.base = sems_s, sems_r, base

        def send(self, peer):
            return put(
                self.source(peer),
                self.target(me),
                self.sems_s.at[self.base + peer],
                self.sems_r.at[self.base + me],
                {"expert": peer},
            )

        def come(self, peer):
            return put(
                self.source(peer),
                self.target(peer),
                self.sems_s.at[self.base + peer],
                self.sems_r.at[self.base + peer],
                {"expert": peer},
            )

        def own(self):
            return pltpu.make_async_copy(
                self.source(me), self.target(me), self.sems_r.at[self.base + me]
            )

        def start(self):
            for peer in peers:
                self.send(peer).start()
            self.own().start()

        def sent(self):
            for peer in peers:
                self.send(peer).wait_send()

        def all_in(self):
            for peer in peers:
                self.come(peer).wait_recv()
            self.own().wait()

    def blocks(ref):
        return lambda e: ref.at[rows_at(e, capacity)]

    swap_rows = Swap(blocks(send_rows), blocks(rows_in), rows_s, rows_r)
    swap_grads = Swap(blocks(send_grads), blocks(grads_in), grads_s, grads_r)
    eo, rg = send_rows, send_grads
    swap_eo = Swap(blocks(eo), blocks(ret_eo), eo_s, eo_r)
    swap_rg = Swap(blocks(rg), blocks(ret_rg), rg_s, rg_r)

    def onehots(plane):
        return [(slot[k] - plane * chunk == slot_lane).astype(F32).astype(BF16) for k in range(2)]

    first = True
    at = 0
    for dz in (2, 1, 3, 0):
        plane = rem(z + dz, NZ)
        hot = onehots(plane)
        send_rows[rows_at(plane, chunk), :] = dot(hot[0] + hot[1], tok_ref[...], 0, 0).astype(BF16)
        if first:
            pl.semaphore_wait(barrier, len(peers) + 3)
            first = False
        number = PLANE - (dz == 0)
        for peer in peers[at : at + number]:
            swap_rows.send(peer).start()
        at += number
    swap_rows.own().start()
    for k in range(2):
        scaled[k * tok : (k + 1) * tok, :] = (
            rw_ref[:, k : k + 1] * og_ref[...].astype(F32)
        ).astype(BF16)
    at = 0
    for dz in (2, 1, 3, 0):
        plane = rem(z + dz, NZ)
        hot = jnp.concatenate(onehots(plane), axis=0)
        send_grads[rows_at(plane, chunk), :] = dot(hot, scaled[...], 0, 0).astype(BF16)
        number = PLANE - (dz == 0)
        for peer in peers[at : at + number]:
            swap_grads.send(peer).start()
        at += number
    swap_grads.own().start()

    for copy in w_copies:
        copy.wait()

    def plane_of(step):
        return rem(z + step + div(step, 2) * (1 - 2 * rem(step, 2)), NZ)

    def forward(step, carry):
        plane = plane_of(step)
        for j in range(PLANE):
            swap_rows.come(plane * PLANE + j).wait_recv()
        at_rows = rows_at(plane, chunk)
        rows = rows_in[at_rows, :]
        gate = dot(rows, w[0])
        up = dot(rows, w[1])
        sig = jax.nn.sigmoid(gate)
        silu = gate * sig
        hidden[at_rows, :] = (silu * up).astype(BF16)
        coef_up[at_rows, :] = silu
        coef_gate[at_rows, :] = up * sig * (1.0 + gate * (1.0 - sig))
        return carry

    lax.fori_loop(0, NZ, forward, 0)
    swap_rows.sent()

    def forward_out(step, carry):
        at_rows = rows_at(step, chunk)
        eo[at_rows, :] = dot(hidden[at_rows, :], w[2], 1, 1).astype(BF16)
        return carry

    lax.fori_loop(0, NZ, forward_out, 0)

    def backward(step, carry):
        plane = plane_of(step)
        for j in range(PLANE):
            swap_grads.come(plane * PLANE + j).wait_recv()
        at_rows = rows_at(plane, chunk)
        hidden_grad = dot(grads_in[at_rows, :], w[2])
        gate_grad[at_rows, :] = (hidden_grad * coef_gate[at_rows, :]).astype(BF16)
        up_grad[at_rows, :] = (hidden_grad * coef_up[at_rows, :]).astype(BF16)
        return carry

    lax.fori_loop(0, NZ, backward, 0)
    swap_eo.start()

    def shard(p, xx, h, cols):
        return pg.at[p, rows_at(xx * 2 + h, half), cols]

    early, late, across = [], [], []
    for i, (p, c0, nc) in enumerate(chunks):
        cols = pl.ds(c0, nc)
        sems = [(x_s.at[6 * i + j], x_r.at[6 * i + j]) for j in range(6)]
        early.append(
            (
                put(shard(p, xo, 0, cols), one_l.at[p, :, cols], *sems[0], right),
                put(shard(p, xo, 1, cols), one_r.at[p, :, cols], *sems[1], left),
                put(shard(p, xp, 1, cols), two_l.at[p, 1, :, cols], *sems[2], right),
                put(shard(p, xm, 0, cols), two_r.at[p, 0, :, cols], *sems[3], left),
            )
        )
        late.append(
            (
                put(one_l.at[p, :, cols], two_l.at[p, 0, :, cols], *sems[4], right),
                put(one_r.at[p, :, cols], two_r.at[p, 1, :, cols], *sems[5], left),
            )
        )
        across.append(
            put(two_l.at[p, 1 - yl, :, cols], y_in.at[p, :, cols], y_s.at[i], y_r.at[i], beside)
        )
    tile = 256

    def weight_grad(p, lhs, rhs):
        def weight_tile(j, carry):
            at_cols = rows_at(j, tile)
            pg[p, at_cols, :] = dot(lhs[:, at_cols], rhs[...], 0, 0).astype(BF16)
            return carry

        lax.fori_loop(0, width // tile, weight_tile, 0)

    def start(group):
        for copy in group:
            copy.start()

    def arrived(group):
        for copy in group:
            copy.wait_recv()

    block = 32
    steps = half // block

    def rows_of(shard_index, i):
        return pl.ds(pl.multiple_of(shard_index * half + i * block, block), block)

    def pass_on(c):
        p, c0, nc = chunks[c]
        cols = pl.ds(c0, nc)

        def add(i, carry):
            at = rows_at(i, block)
            one_l[p, at, cols] = (
                one_l[p, at, cols].astype(F32) + pg[p, rows_of(xp * 2, i), cols].astype(F32)
            ).astype(BF16)
            one_r[p, at, cols] = (
                one_r[p, at, cols].astype(F32) + pg[p, rows_of(xm * 2 + 1, i), cols].astype(F32)
            ).astype(BF16)
            return carry

        lax.fori_loop(0, steps, add, 0)
        start(late[c])

    def give_other(c):
        p, c0, nc = chunks[c]
        cols = pl.ds(c0, nc)
        other = 1 - yl

        def sum_other(i, carry):
            at = rows_at(i, block)
            two_l[p, other, at, cols] = (
                pg[p, rows_of(x * 2 + other, i), cols].astype(F32)
                + two_l[p, other, at, cols].astype(F32)
                + two_r[p, other, at, cols].astype(F32)
            ).astype(BF16)
            return carry

        lax.fori_loop(0, steps, sum_other, 0)
        across[c].start()

    sixteenth = half // experts

    def at_ref(ref):
        return lambda e: ref.at[e]

    def at_home(c):
        p, c0, nc = chunks[c]
        return lambda e: moved.at[p, e, :, :, pl.ds(c0, nc)]

    spread = [
        Swap(at_ref(stages[c]), at_ref(mids[c]), out_s, out_r, c * experts) for c in range(count)
    ]
    settle = [
        Swap(at_ref(stages[c]), at_home(c), home_s, home_r, c * experts) for c in range(count)
    ]

    def update(c):
        p, c0, nc = chunks[c]
        cols = pl.ds(c0, nc)
        across[c].wait_recv()

        def adamw(k, carry):
            at = rows_at(k, sixteenth)
            at_own = pl.ds(pl.multiple_of(d * half + k * sixteenth, sixteenth), sixteenth)
            at_part = pl.ds(
                pl.multiple_of((x * 2 + yl) * half + k * sixteenth, sixteenth), sixteenth
            )
            grad = (
                pg[p, at_part, cols].astype(F32)
                + two_l[p, yl, at, cols].astype(F32)
                + two_r[p, yl, at, cols].astype(F32)
                + y_in[p, at, cols].astype(F32)
            )
            first_new = beta_first * m_ref[0, p, at, cols].astype(F32) + (1.0 - beta_first) * grad
            second_new = (
                beta_second * v_ref[0, p, at, cols].astype(F32) + (1.0 - beta_second) * grad * grad
            )
            full = w[p, at_own, cols].astype(F32)
            change = (
                first_new * (1.0 / first_fix)
                / (jnp.sqrt(second_new * (1.0 / second_fix)) + adam_epsilon)
                + weight_decay * full
            )
            stages[c][k, 0] = (full - learn_rate * change).astype(BF16)
            stages[c][k, 1] = first_new.astype(BF16)
            stages[c][k, 2] = second_new.astype(BF16)
            return carry

        lax.fori_loop(0, experts, adamw, 0)
        spread[c].start()

    def turn(c):
        spread[c].all_in()
        spread[c].sent()

        def reorder(t, carry):
            stages[c][t] = mids[c][partner_ref[t]]
            return carry

        lax.fori_loop(0, experts, reorder, 0)
        settle[c].start()

    slots = ret_eo.shape[0]
    all_lane = lax.broadcasted_iota(jnp.int32, (tok, slots), 1)
    wide = 512

    def hots():
        return [(slot[k] == all_lane).astype(F32).astype(BF16) for k in range(2)]

    def combine_out():
        swap_eo.all_in()
        hot = jnp.concatenate(hots(), axis=0)
        rw = [rw_ref[:, k : k + 1] for k in range(2)]

        def combine(j, route):
            at = rows_at(j, wide)
            pairs = dot(hot, ret_eo[:, at])
            one, two = pairs[:tok], pairs[tok:]
            moe_ref[:, at] = (rw[0] * one + rw[1] * two).astype(BF16)
            grad = og_ref[:, at].astype(F32)
            return (
                route[0] + jnp.sum(grad * one, axis=1, keepdims=True),
                route[1] + jnp.sum(grad * two, axis=1, keepdims=True),
            )

        zero = jnp.zeros((tok, 1), F32)
        route = lax.fori_loop(0, width // wide, combine, (zero, zero))
        route_ref[:, 0:1] = route[0]
        route_ref[:, 1:2] = route[1]

    def combine_grads():
        swap_rg.all_in()
        hot = hots()
        hot_sum = hot[0] + hot[1]

        def combine(j, carry):
            at = rows_at(j, wide)
            tg_ref[:, at] = dot(hot_sum, ret_rg[:, at]).astype(BF16)
            return carry

        lax.fori_loop(0, width // wide, combine, 0)

    weight_grad(2, grads_in, hidden)
    start(early[0])
    start(early[1])
    weight_grad(0, rows_in, gate_grad)
    weight_grad(1, rows_in, up_grad)
    swap_grads.sent()

    def row_tile(j, carry):
        at_cols = rows_at(j, tile)
        rg[:, at_cols] = (
            dot(gate_grad[...], w[0, at_cols, :], 1, 1) + dot(up_grad[...], w[1, at_cols, :], 1, 1)
        ).astype(BF16)
        return carry

    lax.fori_loop(0, width // tile, row_tile, 0)
    swap_rg.start()

    for i in range(count + 3):
        if i < count:
            arrived(early[i])
            if i + 2 < count:
                start(early[i + 2])
            pass_on(i)
        if 0 <= i - 1 < count:
            arrived(late[i - 1])
            give_other(i - 1)
        if 0 <= i - 2 < count:
            update(i - 2)
        if i == 2:
            combine_out()
        if i == 4:
            combine_grads()
        if 0 <= i - 3 < count:
            turn(i - 3)
    for c in range(count):
        settle[c].all_in()
    for c in range(count):
        settle[c].sent()
        for copy in (*early[c], *late[c], across[c]):
            copy.wait_send()
    swap_eo.sent()
    swap_rg.sent()


def per_device(
    tokens, route_weights, assignment, out_grad, weights, first_moment, second_moment, partner
):
    experts = lax.axis_size("expert")
    tok, topk = assignment.shape
    width = tokens.shape[1]
    capacity = 2 * tok * topk // experts
    slots = experts * capacity
    ff = weights.shape[3]
    half = first_moment.shape[2]
    vmem = pl.BlockSpec(memory_space=pltpu.VMEM)
    anywhere = pl.BlockSpec(memory_space=pl.ANY)
    dma = pltpu.SemaphoreType.DMA
    shape = jax.ShapeDtypeStruct
    piece = (3, half, ff)
    sixteenth = half // experts
    cut = ff // 2
    chunks = tuple((p, c0, cut) for p in (2, 0, 1) for c0 in (0, cut))
    sides = [pltpu.VMEM((experts, 3, sixteenth, nc), BF16) for _, _, nc in chunks]
    count = len(chunks)
    wide = pltpu.VMEM((slots, width), BF16)
    moe_out, token_grads, route_grads, moved = pl.pallas_call(
        functools.partial(layer_kernel, capacity, chunks),
        out_shape=(
            shape((tok, width), BF16),
            shape((tok, width), BF16),
            shape((tok, topk), F32),
            shape((3, experts, 3, sixteenth, ff), BF16),
        ),
        in_specs=[pl.BlockSpec(memory_space=pltpu.SMEM)] + [vmem] * 4 + [anywhere] + [vmem] * 2,
        out_specs=(vmem, vmem, vmem, anywhere),
        scratch_shapes=[
            pltpu.VMEM((topk * tok, width), BF16),
            wide,
            wide,
            wide,
            wide,
            pltpu.VMEM((3, width, ff), BF16),
            pltpu.VMEM((slots, ff), F32),
            pltpu.VMEM((slots, ff), F32),
            pltpu.VMEM((slots, ff), BF16),
            pltpu.VMEM((slots, ff), BF16),
            pltpu.VMEM((slots, ff), BF16),
            pltpu.VMEM((3, width, ff), BF16),
            wide,
            wide,
            pltpu.VMEM(piece, BF16),
            pltpu.VMEM(piece, BF16),
            pltpu.VMEM((3, 2, half, ff), BF16),
            pltpu.VMEM((3, 2, half, ff), BF16),
            pltpu.VMEM(piece, BF16),
            *sides,
            *sides,
            dma((3,)),
            *[dma((experts,))] * 8,
            dma((6 * count,)),
            dma((6 * count,)),
            dma((count,)),
            dma((count,)),
            *[dma((count * experts,))] * 4,
        ],
        compiler_params=pltpu.CompilerParams(
            collective_id=0, has_side_effects=True, vmem_limit_bytes=62 * 2**20
        ),
    )(
        partner,
        assignment,
        route_weights,
        tokens,
        out_grad,
        weights,
        first_moment,
        second_moment,
    )
    new = [moved[:, :, k].reshape((1,) + piece) for k in range(3)]
    return (moe_out, token_grads, route_grads, *new)


def solution(mesh):
    placed = (
        P(("expert", "dp"), None),
        P(("expert", "dp"), None),
        P(("expert", "dp"), None),
        P(("expert", "dp"), None),
        P("expert", None, None, None),
        P("expert", None, "dp", None),
        P("expert", None, "dp", None),
        P(),
    )
    return jax.shard_map(
        per_device,
        mesh=mesh,
        in_specs=placed,
        out_specs=(
            P(("expert", "dp"), None),
            P(("expert", "dp"), None),
            P(("expert", "dp"), None),
            P("expert", None, "dp", None),
            P("expert", None, "dp", None),
            P("expert", None, "dp", None),
        ),
        check_vma=False,
    )
```

```python
import functools

import jax
import jax.numpy as jnp
from jax import lax
from jax.experimental import pallas as pl
from jax.experimental.pallas import tpu as pltpu
from jax.sharding import PartitionSpec as P

beta_first = 0.9
beta_second = 0.95
learn_rate = 0.001
weight_decay = 0.1
adam_epsilon = 1e-08
first_fix = 0.9999734386011124
second_fix = 0.994079470779666

MESH = pl.DeviceIdType.MESH
F32 = jnp.float32
BF16 = jnp.bfloat16
LANES = 128
NZ, NY, NC = 4, 2, 2
NX = 4
PLANE = NY * NC


def dot(a, b, ca=1, cb=0):
    return lax.dot_general(a, b, (((ca,), (cb,)), ((), ())), preferred_element_type=F32)


def pair_slots(assigned, capacity):
    tok = assigned[0].shape[0]
    lane = lax.broadcasted_iota(jnp.int32, (tok, LANES), 1)
    named = [(assigned[k] == lane).astype(F32) for k in range(2)]
    below = (
        lax.broadcasted_iota(jnp.int32, (tok, tok), 0)
        > lax.broadcasted_iota(jnp.int32, (tok, tok), 1)
    ).astype(F32)
    earlier = dot(below.astype(BF16), (named[0] + named[1]).astype(BF16))
    return [
        assigned[k] * capacity
        + jnp.sum(earlier * named[k], axis=1, keepdims=True).astype(jnp.int32)
        for k in range(2)
    ]


def rem(a, n):
    return lax.rem(a, jnp.int32(n))


def div(a, n):
    return lax.div(a, jnp.int32(n))


def rows_at(index, size):
    return pl.ds(pl.multiple_of(index * size, size), size)


def expert_coords():
    me = lax.axis_index("expert").astype(jnp.int32)
    return me, div(me, PLANE), rem(div(me, NC), NY), rem(me, NC)


def expert_peers():
    me, z, y, core = expert_coords()
    out = []
    for dz in (2, 1, 3, 0):
        for dy in (1, 0):
            for dc in (0, 1):
                if (dz, dy, dc) != (0, 0, 0):
                    out.append(
                        rem(z + dz, NZ) * PLANE + rem(y + dy, NY) * NC + rem(core + dc, NC)
                    )
    return out


def layer_kernel(
    capacity,
    chunks,
    partner_ref,
    pair_ref,
    tok_ref,
    og_ref,
    w_hbm,
    m_hbm,
    v_hbm,
    moe_ref,
    tg_ref,
    route_ref,
    moved,
    scaled,
    send_rows,
    send_grads,
    rows_in,
    grads_in,
    w,
    coef_gate,
    coef_up,
    hidden,
    gate_grad,
    up_grad,
    pg,
    ret_eo,
    ret_rg,
    one_l,
    one_r,
    two_l,
    two_r,
    y_in,
    m_ref,
    v_ref,
    *rest,
):
    count = len(chunks)
    stages, mids = rest[:count], rest[count : 2 * count]
    (
        w_sem,
        rows_s,
        rows_r,
        grads_s,
        grads_r,
        eo_s,
        eo_r,
        rg_s,
        rg_r,
        x_s,
        x_r,
        y_s,
        y_r,
        out_s,
        out_r,
        home_s,
        home_r,
    ) = rest[2 * count :]
    me, z, y, core = expert_coords()
    d = lax.axis_index("dp").astype(jnp.int32)
    x, yl = div(d, 2), rem(d, 2)
    xp, xm, xo = rem(x + 1, NX), rem(x + NX - 1, NX), rem(x + 2, NX)
    right, left, beside = {"dp": xp * 2 + yl}, {"dp": xm * 2 + yl}, {"dp": x * 2 + 1 - yl}
    tok, width = tok_ref.shape
    experts = stages[0].shape[0]
    half = m_ref.shape[1]
    chunk = PLANE * capacity
    peers = expert_peers()
    barrier = pltpu.get_barrier_semaphore()
    for target in [{"expert": peer} for peer in peers] + [right, left, beside]:
        pl.semaphore_signal(barrier, inc=1, device_id=target, device_id_type=MESH)
    w_copies = [pltpu.make_async_copy(w_hbm.at[0, p], w.at[p], w_sem.at[p]) for p in range(3)]
    w_copies.append(pltpu.make_async_copy(m_hbm.at[0], m_ref, w_sem.at[3]))
    w_copies.append(pltpu.make_async_copy(v_hbm.at[0], v_ref, w_sem.at[4]))
    for copy in w_copies:
        copy.start()

    rw = [pair_ref[:, k : k + 1] for k in range(2)]
    slot = pair_slots([pair_ref[:, k + 2 : k + 3].astype(jnp.int32) for k in range(2)], capacity)
    slot_lane = lax.broadcasted_iota(jnp.int32, (tok, chunk), 1)

    def put(src, dst, sem_s, sem_r, target):
        return pltpu.make_async_remote_copy(
            src_ref=src,
            dst_ref=dst,
            send_sem=sem_s,
            recv_sem=sem_r,
            device_id=target,
            device_id_type=MESH,
        )

    class Swap:
        def __init__(self, source, target, sems_s, sems_r, base=0):
            self.source, self.target = source, target
            self.sems_s, self.sems_r, self.base = sems_s, sems_r, base

        def send(self, peer):
            return put(
                self.source(peer),
                self.target(me),
                self.sems_s.at[self.base + peer],
                self.sems_r.at[self.base + me],
                {"expert": peer},
            )

        def come(self, peer):
            return put(
                self.source(peer),
                self.target(peer),
                self.sems_s.at[self.base + peer],
                self.sems_r.at[self.base + peer],
                {"expert": peer},
            )

        def own(self):
            return pltpu.make_async_copy(
                self.source(me), self.target(me), self.sems_r.at[self.base + me]
            )

        def start(self):
            for peer in peers:
                self.send(peer).start()
            self.own().start()

        def sent(self):
            for peer in peers:
                self.send(peer).wait_send()

        def all_in(self):
            for peer in peers:
                self.come(peer).wait_recv()
            self.own().wait()

    def blocks(ref):
        return lambda e: ref.at[rows_at(e, capacity)]

    swap_rows = Swap(blocks(send_rows), blocks(rows_in), rows_s, rows_r)
    swap_grads = Swap(blocks(send_grads), blocks(grads_in), grads_s, grads_r)
    eo, rg = send_rows, send_grads
    swap_eo = Swap(blocks(eo), blocks(ret_eo), eo_s, eo_r)
    swap_rg = Swap(blocks(rg), blocks(ret_rg), rg_s, rg_r)

    def onehots(plane):
        return [(slot[k] - plane * chunk == slot_lane).astype(F32).astype(BF16) for k in range(2)]

    first = True
    at = 0
    for dz in (2, 1, 3, 0):
        plane = rem(z + dz, NZ)
        hot = onehots(plane)
        send_rows[rows_at(plane, chunk), :] = dot(hot[0] + hot[1], tok_ref[...], 0, 0).astype(BF16)
        if first:
            pl.semaphore_wait(barrier, len(peers) + 3)
            first = False
        number = PLANE - (dz == 0)
        for peer in peers[at : at + number]:
            swap_rows.send(peer).start()
        at += number
    swap_rows.own().start()
    for k in range(2):
        scaled[k * tok : (k + 1) * tok, :] = (
            rw[k] * og_ref[...].astype(F32)
        ).astype(BF16)
    for dz in range(NZ):
        hot = jnp.concatenate(onehots(dz), axis=0)
        send_grads[dz * chunk : (dz + 1) * chunk, :] = dot(hot, scaled[...], 0, 0).astype(BF16)

    for copy in w_copies:
        copy.wait()

    swap_rows.all_in()
    swap_grads.start()
    ffs = w.shape[2]
    tile = 256

    def forward(j, carry):
        at_cols = rows_at(j, tile)
        rows = rows_in[...]
        gate = dot(rows, w[0, :, at_cols])
        up = dot(rows, w[1, :, at_cols])
        sig = jax.nn.sigmoid(gate)
        silu = gate * sig
        hidden[:, at_cols] = (silu * up).astype(BF16)
        coef_up[:, at_cols] = silu
        coef_gate[:, at_cols] = up * sig * (1.0 + gate * (1.0 - sig))
        return carry

    lax.fori_loop(0, ffs // tile, forward, 0)
    swap_rows.sent()

    def forward_out(j, carry):
        at_cols = rows_at(j, tile)
        eo[:, at_cols] = dot(hidden[...], w[2, at_cols, :], 1, 1).astype(BF16)
        return carry

    lax.fori_loop(0, width // tile, forward_out, 0)
    swap_grads.all_in()
    swap_eo.start()

    def shard(p, xx, h, cols):
        return pg.at[p, rows_at(xx * 2 + h, half), cols]

    early, late, across = [], [], []
    for i, (p, c0, nc) in enumerate(chunks):
        cols = pl.ds(c0, nc)
        sems = [(x_s.at[6 * i + j], x_r.at[6 * i + j]) for j in range(6)]
        early.append(
            (
                put(shard(p, xo, 0, cols), one_l.at[p, :, cols], *sems[0], right),
                put(shard(p, xo, 1, cols), one_r.at[p, :, cols], *sems[1], left),
                put(shard(p, xp, 1, cols), two_l.at[p, 1, :, cols], *sems[2], right),
                put(shard(p, xm, 0, cols), two_r.at[p, 0, :, cols], *sems[3], left),
            )
        )
        late.append(
            (
                put(one_l.at[p, :, cols], two_l.at[p, 0, :, cols], *sems[4], right),
                put(one_r.at[p, :, cols], two_r.at[p, 1, :, cols], *sems[5], left),
            )
        )
        across.append(
            put(two_l.at[p, 1 - yl, :, cols], y_in.at[p, :, cols], y_s.at[i], y_r.at[i], beside)
        )

    def weight_grad(p, lhs, rhs):
        def weight_tile(j, carry):
            at_cols = rows_at(j, tile)
            pg[p, at_cols, :] = dot(lhs[:, at_cols], rhs[...], 0, 0).astype(BF16)
            return carry

        lax.fori_loop(0, width // tile, weight_tile, 0)

    def start(group):
        for copy in group:
            copy.start()

    def arrived(group):
        for copy in group:
            copy.wait_recv()

    block = 32
    steps = half // block

    def rows_of(shard_index, i):
        return pl.ds(pl.multiple_of(shard_index * half + i * block, block), block)

    def pass_on(c):
        p, c0, nc = chunks[c]
        cols = pl.ds(c0, nc)

        def add(i, carry):
            at = rows_at(i, block)
            one_l[p, at, cols] = (
                one_l[p, at, cols].astype(F32) + pg[p, rows_of(xp * 2, i), cols].astype(F32)
            ).astype(BF16)
            one_r[p, at, cols] = (
                one_r[p, at, cols].astype(F32) + pg[p, rows_of(xm * 2 + 1, i), cols].astype(F32)
            ).astype(BF16)
            return carry

        lax.fori_loop(0, steps, add, 0)
        start(late[c])

    def give_other(c):
        p, c0, nc = chunks[c]
        cols = pl.ds(c0, nc)
        other = 1 - yl

        def sum_other(i, carry):
            at = rows_at(i, block)
            two_l[p, other, at, cols] = (
                pg[p, rows_of(x * 2 + other, i), cols].astype(F32)
                + two_l[p, other, at, cols].astype(F32)
                + two_r[p, other, at, cols].astype(F32)
            ).astype(BF16)
            return carry

        lax.fori_loop(0, steps, sum_other, 0)
        across[c].start()

    sixteenth = half // experts

    def at_ref(ref):
        return lambda e: ref.at[e]

    def at_home(c):
        p, c0, nc = chunks[c]
        return lambda e: moved.at[p, e, :, :, pl.ds(c0, nc)]

    spread = [
        Swap(at_ref(stages[c]), at_ref(mids[c]), out_s, out_r, c * experts) for c in range(count)
    ]
    settle = [
        Swap(at_ref(stages[c]), at_home(c), home_s, home_r, c * experts) for c in range(count)
    ]

    def update(c):
        p, c0, nc = chunks[c]
        cols = pl.ds(c0, nc)
        across[c].wait_recv()

        def adamw(k, carry):
            at = rows_at(k, sixteenth)
            at_own = pl.ds(pl.multiple_of(d * half + k * sixteenth, sixteenth), sixteenth)
            at_part = pl.ds(
                pl.multiple_of((x * 2 + yl) * half + k * sixteenth, sixteenth), sixteenth
            )
            grad = (
                pg[p, at_part, cols].astype(F32)
                + two_l[p, yl, at, cols].astype(F32)
                + two_r[p, yl, at, cols].astype(F32)
                + y_in[p, at, cols].astype(F32)
            )
            first_new = beta_first * m_ref[p, at, cols].astype(F32) + (1.0 - beta_first) * grad
            second_new = (
                beta_second * v_ref[p, at, cols].astype(F32) + (1.0 - beta_second) * grad * grad
            )
            full = w[p, at_own, cols].astype(F32)
            change = (
                first_new * (1.0 / first_fix)
                / (jnp.sqrt(second_new * (1.0 / second_fix)) + adam_epsilon)
                + weight_decay * full
            )
            stages[c][k, 0] = (full - learn_rate * change).astype(BF16)
            stages[c][k, 1] = first_new.astype(BF16)
            stages[c][k, 2] = second_new.astype(BF16)
            return carry

        lax.fori_loop(0, experts, adamw, 0)
        spread[c].start()

    def turn(c):
        spread[c].all_in()
        spread[c].sent()

        def reorder(t, carry):
            stages[c][t] = mids[c][partner_ref[t]]
            return carry

        lax.fori_loop(0, experts, reorder, 0)
        settle[c].start()

    slots = ret_eo.shape[0]
    all_lane = lax.broadcasted_iota(jnp.int32, (tok, slots), 1)
    wide = 512

    def hots():
        return [(slot[k] == all_lane).astype(F32).astype(BF16) for k in range(2)]

    def combine_out():
        swap_eo.all_in()
        hot = jnp.concatenate(hots(), axis=0)

        def combine(j, route):
            at = rows_at(j, wide)
            pairs = dot(hot, ret_eo[:, at])
            one, two = pairs[:tok], pairs[tok:]
            moe_ref[:, at] = (rw[0] * one + rw[1] * two).astype(BF16)
            grad = og_ref[:, at].astype(F32)
            return (
                route[0] + jnp.sum(grad * one, axis=1, keepdims=True),
                route[1] + jnp.sum(grad * two, axis=1, keepdims=True),
            )

        zero = jnp.zeros((tok, 1), F32)
        route = lax.fori_loop(0, width // wide, combine, (zero, zero))
        route_ref[:, 0:1] = route[0]
        route_ref[:, 1:2] = route[1]

    def combine_grads():
        swap_rg.all_in()
        hot = hots()
        hot_sum = hot[0] + hot[1]

        def combine(j, carry):
            at = rows_at(j, wide)
            tg_ref[:, at] = dot(hot_sum, ret_rg[:, at]).astype(BF16)
            return carry

        lax.fori_loop(0, width // wide, combine, 0)

    weight_grad(2, grads_in, hidden)
    start(early[0])

    def backward(j, carry):
        at_cols = rows_at(j, tile)
        hidden_grad = dot(grads_in[...], w[2, :, at_cols])
        gate_grad[:, at_cols] = (hidden_grad * coef_gate[:, at_cols]).astype(BF16)
        up_grad[:, at_cols] = (hidden_grad * coef_up[:, at_cols]).astype(BF16)
        return carry

    lax.fori_loop(0, ffs // tile, backward, 0)
    start(early[1])
    weight_grad(0, rows_in, gate_grad)
    weight_grad(1, rows_in, up_grad)
    swap_grads.sent()

    def row_tile(j, carry):
        at_cols = rows_at(j, tile)
        rg[:, at_cols] = (
            dot(gate_grad[...], w[0, at_cols, :], 1, 1) + dot(up_grad[...], w[1, at_cols, :], 1, 1)
        ).astype(BF16)
        return carry

    lax.fori_loop(0, width // tile, row_tile, 0)
    swap_rg.start()

    def first_leg(c):
        arrived(early[c])
        if c + 2 < count:
            start(early[c + 2])
        pass_on(c)

    def second_leg(c):
        arrived(late[c])
        give_other(c)

    first_leg(0)
    first_leg(1)
    combine_out()
    second_leg(0)
    first_leg(2)
    second_leg(1)
    first_leg(3)
    update(0)
    second_leg(2)
    first_leg(4)
    update(1)
    turn(0)
    combine_grads()
    second_leg(3)
    first_leg(5)
    update(2)
    turn(1)
    second_leg(4)
    update(3)
    turn(2)
    second_leg(5)
    update(4)
    turn(3)
    update(5)
    turn(4)
    turn(5)
    for c in range(count):
        settle[c].all_in()
    for c in range(count):
        settle[c].sent()
        for copy in (*early[c], *late[c], across[c]):
            copy.wait_send()
    swap_eo.sent()
    swap_rg.sent()


def per_device(
    tokens, route_weights, assignment, out_grad, weights, first_moment, second_moment, partner
):
    experts = lax.axis_size("expert")
    tok, topk = assignment.shape
    width = tokens.shape[1]
    capacity = 2 * tok * topk // experts
    slots = experts * capacity
    ff = weights.shape[3]
    half = first_moment.shape[2]
    vmem = pl.BlockSpec(memory_space=pltpu.VMEM)
    anywhere = pl.BlockSpec(memory_space=pl.ANY)
    dma = pltpu.SemaphoreType.DMA
    shape = jax.ShapeDtypeStruct
    piece = (3, half, ff)
    sixteenth = half // experts
    cut = ff // 2
    chunks = tuple((p, c0, cut) for p in (2, 0, 1) for c0 in (0, cut))
    sides = [pltpu.VMEM((experts, 3, sixteenth, nc), BF16) for _, _, nc in chunks]
    count = len(chunks)
    wide = pltpu.VMEM((slots, width), BF16)
    moe_out, token_grads, route_grads, moved = pl.pallas_call(
        functools.partial(layer_kernel, capacity, chunks),
        out_shape=(
            shape((tok, width), BF16),
            shape((tok, width), BF16),
            shape((tok, topk), F32),
            shape((3, experts, 3, sixteenth, ff), BF16),
        ),
        in_specs=[pl.BlockSpec(memory_space=pltpu.SMEM)] + [vmem] * 3 + [anywhere] * 3,
        out_specs=(vmem, vmem, vmem, anywhere),
        scratch_shapes=[
            pltpu.VMEM((topk * tok, width), BF16),
            wide,
            wide,
            wide,
            wide,
            pltpu.VMEM((3, width, ff), BF16),
            pltpu.VMEM((slots, ff), F32),
            pltpu.VMEM((slots, ff), F32),
            pltpu.VMEM((slots, ff), BF16),
            pltpu.VMEM((slots, ff), BF16),
            pltpu.VMEM((slots, ff), BF16),
            pltpu.VMEM((3, width, ff), BF16),
            wide,
            wide,
            pltpu.VMEM(piece, BF16),
            pltpu.VMEM(piece, BF16),
            pltpu.VMEM((3, 2, half, ff), BF16),
            pltpu.VMEM((3, 2, half, ff), BF16),
            pltpu.VMEM(piece, BF16),
            pltpu.VMEM(piece, BF16),
            pltpu.VMEM(piece, BF16),
            *sides,
            *sides,
            dma((5,)),
            *[dma((experts,))] * 8,
            dma((6 * count,)),
            dma((6 * count,)),
            dma((count,)),
            dma((count,)),
            *[dma((count * experts,))] * 4,
        ],
        compiler_params=pltpu.CompilerParams(
            collective_id=0, has_side_effects=True, vmem_limit_bytes=62 * 2**20
        ),
    )(
        partner,
        jnp.concatenate([route_weights, assignment.astype(F32)], axis=1),
        tokens,
        out_grad,
        weights,
        first_moment,
        second_moment,
    )
    new = [moved[:, :, k].reshape((1,) + piece) for k in range(3)]
    return (moe_out, token_grads, route_grads, *new)


def solution(mesh):
    placed = (
        P(("expert", "dp"), None),
        P(("expert", "dp"), None),
        P(("expert", "dp"), None),
        P(("expert", "dp"), None),
        P("expert", None, None, None),
        P("expert", None, "dp", None),
        P("expert", None, "dp", None),
        P(),
    )
    return jax.shard_map(
        per_device,
        mesh=mesh,
        in_specs=placed,
        out_specs=(
            P(("expert", "dp"), None),
            P(("expert", "dp"), None),
            P(("expert", "dp"), None),
            P("expert", None, "dp", None),
            P("expert", None, "dp", None),
            P("expert", None, "dp", None),
        ),
        check_vma=False,
    )
```

```python
import functools

import jax
import jax.numpy as jnp
from jax import lax
from jax.experimental import pallas as pl
from jax.experimental.pallas import tpu as pltpu
from jax.sharding import PartitionSpec as P

beta_first = 0.9
beta_second = 0.95
learn_rate = 0.001
weight_decay = 0.1
adam_epsilon = 1e-08
first_fix = 0.9999734386011124
second_fix = 0.994079470779666

MESH = pl.DeviceIdType.MESH
F32 = jnp.float32
BF16 = jnp.bfloat16
LANES = 128
NZ, NY, NC = 4, 2, 2
NX = 4
PLANE = NY * NC


def dot(a, b, ca=1, cb=0):
    return lax.dot_general(a, b, (((ca,), (cb,)), ((), ())), preferred_element_type=F32)


def pair_slots(assigned, capacity):
    tok = assigned[0].shape[0]
    lane = lax.broadcasted_iota(jnp.int32, (tok, LANES), 1)
    named = [(assigned[k] == lane).astype(F32) for k in range(2)]
    below = (
        lax.broadcasted_iota(jnp.int32, (tok, tok), 0)
        > lax.broadcasted_iota(jnp.int32, (tok, tok), 1)
    ).astype(F32)
    earlier = dot(below.astype(BF16), (named[0] + named[1]).astype(BF16))
    return [
        assigned[k] * capacity
        + jnp.sum(earlier * named[k], axis=1, keepdims=True).astype(jnp.int32)
        for k in range(2)
    ]


def rem(a, n):
    return lax.rem(a, jnp.int32(n))


def div(a, n):
    return lax.div(a, jnp.int32(n))


def rows_at(index, size):
    return pl.ds(pl.multiple_of(index * size, size), size)


def expert_coords():
    me = lax.axis_index("expert").astype(jnp.int32)
    return me, div(me, PLANE), rem(div(me, NC), NY), rem(me, NC)


def expert_peers():
    me, z, y, core = expert_coords()
    out = []
    for dz in (2, 1, 3, 0):
        for dy in (1, 0):
            for dc in (0, 1):
                if (dz, dy, dc) != (0, 0, 0):
                    out.append(
                        rem(z + dz, NZ) * PLANE + rem(y + dy, NY) * NC + rem(core + dc, NC)
                    )
    return out


def layer_kernel(
    capacity,
    chunks,
    partner_ref,
    pair_ref,
    tok_ref,
    og_ref,
    w_hbm,
    m_hbm,
    v_hbm,
    moe_ref,
    tg_ref,
    route_ref,
    moved,
    scaled,
    send_rows,
    send_grads,
    rows_in,
    grads_in,
    w,
    coef_gate,
    coef_up,
    hidden,
    gate_grad,
    up_grad,
    pg,
    ret_eo,
    ret_rg,
    one_l,
    one_r,
    two_l,
    two_r,
    y_in,
    m_ref,
    v_ref,
    *rest,
):
    count = len(chunks)
    stages, mids = rest[:count], rest[count : 2 * count]
    (
        w_sem,
        rows_s,
        rows_r,
        grads_s,
        grads_r,
        eo_s,
        eo_r,
        rg_s,
        rg_r,
        x_s,
        x_r,
        y_s,
        y_r,
        out_s,
        out_r,
        home_s,
        home_r,
    ) = rest[2 * count :]
    me, z, y, core = expert_coords()
    d = lax.axis_index("dp").astype(jnp.int32)
    x, yl = div(d, 2), rem(d, 2)
    xp, xm, xo = rem(x + 1, NX), rem(x + NX - 1, NX), rem(x + 2, NX)
    right, left, beside = {"dp": xp * 2 + yl}, {"dp": xm * 2 + yl}, {"dp": x * 2 + 1 - yl}
    tok, width = tok_ref.shape
    experts = stages[0].shape[0]
    half = m_ref.shape[1]
    chunk = PLANE * capacity
    peers = expert_peers()
    barrier = pltpu.get_barrier_semaphore()
    for target in [{"expert": peer} for peer in peers] + [right, left, beside]:
        pl.semaphore_signal(barrier, inc=1, device_id=target, device_id_type=MESH)
    w_copies = [pltpu.make_async_copy(w_hbm.at[0, p], w.at[p], w_sem.at[p]) for p in range(3)]
    w_copies.append(pltpu.make_async_copy(m_hbm.at[0], m_ref, w_sem.at[3]))
    w_copies.append(pltpu.make_async_copy(v_hbm.at[0], v_ref, w_sem.at[4]))
    for copy in w_copies:
        copy.start()

    rw = [pair_ref[:, k : k + 1] for k in range(2)]
    slot = pair_slots([pair_ref[:, k + 2 : k + 3].astype(jnp.int32) for k in range(2)], capacity)
    slot_lane = lax.broadcasted_iota(jnp.int32, (tok, chunk), 1)

    def put(src, dst, sem_s, sem_r, target):
        return pltpu.make_async_remote_copy(
            src_ref=src,
            dst_ref=dst,
            send_sem=sem_s,
            recv_sem=sem_r,
            device_id=target,
            device_id_type=MESH,
        )

    class Swap:
        def __init__(self, source, target, sems_s, sems_r, base=0):
            self.source, self.target = source, target
            self.sems_s, self.sems_r, self.base = sems_s, sems_r, base

        def send(self, peer):
            return put(
                self.source(peer),
                self.target(me),
                self.sems_s.at[self.base + peer],
                self.sems_r.at[self.base + me],
                {"expert": peer},
            )

        def come(self, peer):
            return put(
                self.source(peer),
                self.target(peer),
                self.sems_s.at[self.base + peer],
                self.sems_r.at[self.base + peer],
                {"expert": peer},
            )

        def own(self):
            return pltpu.make_async_copy(
                self.source(me), self.target(me), self.sems_r.at[self.base + me]
            )

        def start(self):
            for peer in peers:
                self.send(peer).start()
            self.own().start()

        def sent(self):
            for peer in peers:
                self.send(peer).wait_send()

        def all_in(self):
            for peer in peers:
                self.come(peer).wait_recv()
            self.own().wait()

    def blocks(ref):
        return lambda e: ref.at[rows_at(e, capacity)]

    swap_rows = Swap(blocks(send_rows), blocks(rows_in), rows_s, rows_r)
    swap_grads = Swap(blocks(send_grads), blocks(grads_in), grads_s, grads_r)
    eo, rg = send_rows, send_grads
    swap_eo = Swap(blocks(eo), blocks(ret_eo), eo_s, eo_r)
    swap_rg = Swap(blocks(rg), blocks(ret_rg), rg_s, rg_r)

    def onehots(plane):
        return [(slot[k] - plane * chunk == slot_lane).astype(F32).astype(BF16) for k in range(2)]

    first = True
    at = 0
    for dz in (2, 1, 3, 0):
        plane = rem(z + dz, NZ)
        hot = onehots(plane)
        send_rows[rows_at(plane, chunk), :] = dot(hot[0] + hot[1], tok_ref[...], 0, 0).astype(BF16)
        if first:
            pl.semaphore_wait(barrier, len(peers) + 3)
            first = False
        number = PLANE - (dz == 0)
        for peer in peers[at : at + number]:
            swap_rows.send(peer).start()
        at += number
    swap_rows.own().start()
    for k in range(2):
        scaled[k * tok : (k + 1) * tok, :] = (
            rw[k] * og_ref[...].astype(F32)
        ).astype(BF16)
    for dz in range(NZ):
        hot = jnp.concatenate(onehots(dz), axis=0)
        send_grads[dz * chunk : (dz + 1) * chunk, :] = dot(hot, scaled[...], 0, 0).astype(BF16)

    for copy in w_copies:
        copy.wait()

    near = len(peers) // 2
    for peer in peers[near:]:
        swap_rows.come(peer).wait_recv()
    swap_grads.start()
    for peer in peers[:near]:
        swap_rows.come(peer).wait_recv()
    swap_rows.own().wait()
    ffs = w.shape[2]
    tile = 256

    def forward(j, carry):
        at_cols = rows_at(j, tile)
        rows = rows_in[...]
        gate = dot(rows, w[0, :, at_cols])
        up = dot(rows, w[1, :, at_cols])
        sig = jax.nn.sigmoid(gate)
        silu = gate * sig
        hidden[:, at_cols] = (silu * up).astype(BF16)
        coef_up[:, at_cols] = silu
        coef_gate[:, at_cols] = up * sig * (1.0 + gate * (1.0 - sig))
        return carry

    lax.fori_loop(0, ffs // tile, forward, 0)
    swap_rows.sent()

    def forward_out(j, carry):
        at_cols = rows_at(j, tile)
        eo[:, at_cols] = dot(hidden[...], w[2, at_cols, :], 1, 1).astype(BF16)
        return carry

    lax.fori_loop(0, width // tile, forward_out, 0)
    swap_grads.all_in()
    swap_eo.start()

    def shard(p, xx, h, cols):
        return pg.at[p, rows_at(xx * 2 + h, half), cols]

    early, late, across = [], [], []
    for i, (p, c0, nc) in enumerate(chunks):
        cols = pl.ds(c0, nc)
        sems = [(x_s.at[6 * i + j], x_r.at[6 * i + j]) for j in range(6)]
        early.append(
            (
                put(shard(p, xo, 0, cols), one_l.at[p, :, cols], *sems[0], right),
                put(shard(p, xo, 1, cols), one_r.at[p, :, cols], *sems[1], left),
                put(shard(p, xp, 1, cols), two_l.at[p, 1, :, cols], *sems[2], right),
                put(shard(p, xm, 0, cols), two_r.at[p, 0, :, cols], *sems[3], left),
            )
        )
        late.append(
            (
                put(one_l.at[p, :, cols], two_l.at[p, 0, :, cols], *sems[4], right),
                put(one_r.at[p, :, cols], two_r.at[p, 1, :, cols], *sems[5], left),
            )
        )
        across.append(
            put(two_l.at[p, 1 - yl, :, cols], y_in.at[p, :, cols], y_s.at[i], y_r.at[i], beside)
        )

    def weight_grad(p, lhs, rhs):
        def weight_tile(j, carry):
            at_cols = rows_at(j, tile)
            pg[p, at_cols, :] = dot(lhs[:, at_cols], rhs[...], 0, 0).astype(BF16)
            return carry

        lax.fori_loop(0, width // tile, weight_tile, 0)

    def start(group):
        for copy in group:
            copy.start()

    def arrived(group):
        for copy in group:
            copy.wait_recv()

    block = 32
    steps = half // block

    def rows_of(shard_index, i):
        return pl.ds(pl.multiple_of(shard_index * half + i * block, block), block)

    def pass_on(c):
        p, c0, nc = chunks[c]
        cols = pl.ds(c0, nc)

        def add(i, carry):
            at = rows_at(i, block)
            one_l[p, at, cols] = (
                one_l[p, at, cols].astype(F32) + pg[p, rows_of(xp * 2, i), cols].astype(F32)
            ).astype(BF16)
            one_r[p, at, cols] = (
                one_r[p, at, cols].astype(F32) + pg[p, rows_of(xm * 2 + 1, i), cols].astype(F32)
            ).astype(BF16)
            return carry

        lax.fori_loop(0, steps, add, 0)
        start(late[c])

    def give_other(c):
        p, c0, nc = chunks[c]
        cols = pl.ds(c0, nc)
        other = 1 - yl

        def sum_other(i, carry):
            at = rows_at(i, block)
            two_l[p, other, at, cols] = (
                pg[p, rows_of(x * 2 + other, i), cols].astype(F32)
                + two_l[p, other, at, cols].astype(F32)
                + two_r[p, other, at, cols].astype(F32)
            ).astype(BF16)
            return carry

        lax.fori_loop(0, steps, sum_other, 0)
        across[c].start()

    sixteenth = half // experts

    def at_ref(ref):
        return lambda e: ref.at[e]

    def at_home(c):
        p, c0, nc = chunks[c]
        return lambda e: moved.at[p, e, :, :, pl.ds(c0, nc)]

    spread = [
        Swap(at_ref(stages[c]), at_ref(mids[c]), out_s, out_r, c * experts) for c in range(count)
    ]
    settle = [
        Swap(at_ref(stages[c]), at_home(c), home_s, home_r, c * experts) for c in range(count)
    ]

    def update(c):
        p, c0, nc = chunks[c]
        cols = pl.ds(c0, nc)
        across[c].wait_recv()

        def adamw(k, carry):
            at = rows_at(k, sixteenth)
            at_own = pl.ds(pl.multiple_of(d * half + k * sixteenth, sixteenth), sixteenth)
            at_part = pl.ds(
                pl.multiple_of((x * 2 + yl) * half + k * sixteenth, sixteenth), sixteenth
            )
            grad = (
                pg[p, at_part, cols].astype(F32)
                + two_l[p, yl, at, cols].astype(F32)
                + two_r[p, yl, at, cols].astype(F32)
                + y_in[p, at, cols].astype(F32)
            )
            first_new = beta_first * m_ref[p, at, cols].astype(F32) + (1.0 - beta_first) * grad
            second_new = (
                beta_second * v_ref[p, at, cols].astype(F32) + (1.0 - beta_second) * grad * grad
            )
            full = w[p, at_own, cols].astype(F32)
            change = (
                first_new * (1.0 / first_fix)
                / (jnp.sqrt(second_new * (1.0 / second_fix)) + adam_epsilon)
                + weight_decay * full
            )
            stages[c][k, 0] = (full - learn_rate * change).astype(BF16)
            stages[c][k, 1] = first_new.astype(BF16)
            stages[c][k, 2] = second_new.astype(BF16)
            return carry

        lax.fori_loop(0, experts, adamw, 0)
        spread[c].start()

    def turn(c):
        spread[c].all_in()
        spread[c].sent()

        def reorder(t, carry):
            stages[c][t] = mids[c][partner_ref[t]]
            return carry

        lax.fori_loop(0, experts, reorder, 0)
        settle[c].start()

    slots = ret_eo.shape[0]
    all_lane = lax.broadcasted_iota(jnp.int32, (tok, slots), 1)
    wide = 512

    def hots():
        return [(slot[k] == all_lane).astype(F32).astype(BF16) for k in range(2)]

    def combine_out():
        swap_eo.all_in()
        hot = jnp.concatenate(hots(), axis=0)

        def combine(j, route):
            at = rows_at(j, wide)
            pairs = dot(hot, ret_eo[:, at])
            one, two = pairs[:tok], pairs[tok:]
            moe_ref[:, at] = (rw[0] * one + rw[1] * two).astype(BF16)
            grad = og_ref[:, at].astype(F32)
            return (
                route[0] + jnp.sum(grad * one, axis=1, keepdims=True),
                route[1] + jnp.sum(grad * two, axis=1, keepdims=True),
            )

        zero = jnp.zeros((tok, 1), F32)
        route = lax.fori_loop(0, width // wide, combine, (zero, zero))
        route_ref[:, 0:1] = route[0]
        route_ref[:, 1:2] = route[1]

    def combine_grads():
        swap_rg.all_in()
        hot = hots()
        hot_sum = hot[0] + hot[1]

        def combine(j, carry):
            at = rows_at(j, wide)
            tg_ref[:, at] = dot(hot_sum, ret_rg[:, at]).astype(BF16)
            return carry

        lax.fori_loop(0, width // wide, combine, 0)

    weight_grad(2, grads_in, hidden)
    start(early[0])

    def backward(j, carry):
        at_cols = rows_at(j, tile)
        hidden_grad = dot(grads_in[...], w[2, :, at_cols])
        gate_grad[:, at_cols] = (hidden_grad * coef_gate[:, at_cols]).astype(BF16)
        up_grad[:, at_cols] = (hidden_grad * coef_up[:, at_cols]).astype(BF16)
        return carry

    lax.fori_loop(0, ffs // tile, backward, 0)
    start(early[1])
    weight_grad(0, rows_in, gate_grad)
    weight_grad(1, rows_in, up_grad)
    swap_grads.sent()

    def row_tile(j, carry):
        at_cols = rows_at(j, tile)
        rg[:, at_cols] = (
            dot(gate_grad[...], w[0, at_cols, :], 1, 1) + dot(up_grad[...], w[1, at_cols, :], 1, 1)
        ).astype(BF16)
        return carry

    lax.fori_loop(0, width // tile, row_tile, 0)
    swap_rg.start()

    def first_leg(c):
        arrived(early[c])
        if c + 2 < count:
            start(early[c + 2])
        pass_on(c)

    def second_leg(c):
        arrived(late[c])
        give_other(c)

    first_leg(0)
    first_leg(1)
    combine_out()
    second_leg(0)
    first_leg(2)
    second_leg(1)
    first_leg(3)
    update(0)
    second_leg(2)
    first_leg(4)
    update(1)
    turn(0)
    combine_grads()
    second_leg(3)
    first_leg(5)
    update(2)
    turn(1)
    second_leg(4)
    update(3)
    turn(2)
    second_leg(5)
    update(4)
    turn(3)
    update(5)
    turn(4)
    turn(5)
    for c in range(count):
        settle[c].all_in()
    for c in range(count):
        settle[c].sent()
        for copy in (*early[c], *late[c], across[c]):
            copy.wait_send()
    swap_eo.sent()
    swap_rg.sent()


def per_device(
    tokens, route_weights, assignment, out_grad, weights, first_moment, second_moment, partner
):
    experts = lax.axis_size("expert")
    tok, topk = assignment.shape
    width = tokens.shape[1]
    capacity = 2 * tok * topk // experts
    slots = experts * capacity
    ff = weights.shape[3]
    half = first_moment.shape[2]
    vmem = pl.BlockSpec(memory_space=pltpu.VMEM)
    anywhere = pl.BlockSpec(memory_space=pl.ANY)
    dma = pltpu.SemaphoreType.DMA
    shape = jax.ShapeDtypeStruct
    piece = (3, half, ff)
    sixteenth = half // experts
    cut = ff // 2
    chunks = tuple((p, c0, cut) for p in (2, 0, 1) for c0 in (0, cut))
    sides = [pltpu.VMEM((experts, 3, sixteenth, nc), BF16) for _, _, nc in chunks]
    count = len(chunks)
    wide = pltpu.VMEM((slots, width), BF16)
    moe_out, token_grads, route_grads, moved = pl.pallas_call(
        functools.partial(layer_kernel, capacity, chunks),
        out_shape=(
            shape((tok, width), BF16),
            shape((tok, width), BF16),
            shape((tok, topk), F32),
            shape((3, experts, 3, sixteenth, ff), BF16),
        ),
        in_specs=[pl.BlockSpec(memory_space=pltpu.SMEM)] + [vmem] * 3 + [anywhere] * 3,
        out_specs=(vmem, vmem, vmem, anywhere),
        scratch_shapes=[
            pltpu.VMEM((topk * tok, width), BF16),
            wide,
            wide,
            wide,
            wide,
            pltpu.VMEM((3, width, ff), BF16),
            pltpu.VMEM((slots, ff), F32),
            pltpu.VMEM((slots, ff), F32),
            pltpu.VMEM((slots, ff), BF16),
            pltpu.VMEM((slots, ff), BF16),
            pltpu.VMEM((slots, ff), BF16),
            pltpu.VMEM((3, width, ff), BF16),
            wide,
            wide,
            pltpu.VMEM(piece, BF16),
            pltpu.VMEM(piece, BF16),
            pltpu.VMEM((3, 2, half, ff), BF16),
            pltpu.VMEM((3, 2, half, ff), BF16),
            pltpu.VMEM(piece, BF16),
            pltpu.VMEM(piece, BF16),
            pltpu.VMEM(piece, BF16),
            *sides,
            *sides,
            dma((5,)),
            *[dma((experts,))] * 8,
            dma((6 * count,)),
            dma((6 * count,)),
            dma((count,)),
            dma((count,)),
            *[dma((count * experts,))] * 4,
        ],
        compiler_params=pltpu.CompilerParams(
            collective_id=0, has_side_effects=True, vmem_limit_bytes=62 * 2**20
        ),
    )(
        partner,
        jnp.concatenate([route_weights, assignment.astype(F32)], axis=1),
        tokens,
        out_grad,
        weights,
        first_moment,
        second_moment,
    )
    new = [moved[:, :, k].reshape((1,) + piece) for k in range(3)]
    return (moe_out, token_grads, route_grads, *new)


def solution(mesh):
    placed = (
        P(("expert", "dp"), None),
        P(("expert", "dp"), None),
        P(("expert", "dp"), None),
        P(("expert", "dp"), None),
        P("expert", None, None, None),
        P("expert", None, "dp", None),
        P("expert", None, "dp", None),
        P(),
    )
    return jax.shard_map(
        per_device,
        mesh=mesh,
        in_specs=placed,
        out_specs=(
            P(("expert", "dp"), None),
            P(("expert", "dp"), None),
            P(("expert", "dp"), None),
            P("expert", None, "dp", None),
            P("expert", None, "dp", None),
            P("expert", None, "dp", None),
        ),
        check_vma=False,
    )
```
